128 devices in a mesh: fsdp: 8 (over z_hi, y), tp: 16 (over x, z_lo, core).
Axes of the slice: x: 4, y: 4, z: 4 (z_hi: 2, z_lo: 2; z = z_hi * 2 + z_lo), core: 2. Of those that a mesh axis runs over, the one named last changes fastest.
Arguments:
- gate_pre: bfloat16 [2048, 26624], P('fsdp', 'tp'), may hold values from -9 to 9
- up_pre: bfloat16 [2048, 26624], P('fsdp', 'tp'), may hold values from -6 to 6
- down_weight: bfloat16 [26624, 8192], P('tp', 'fsdp'), may hold values from -0.0390625 to 0.0390625
- out_grad: bfloat16 [2048, 8192], P(('fsdp', 'tp')), may hold values from -6 to 6
Outputs:
- layer_out: bfloat16 [2048, 8192], P(('fsdp', 'tp'))
- gate_delta: bfloat16 [2048, 26624], P('fsdp', 'tp')
- up_delta: bfloat16 [2048, 26624], P('fsdp', 'tp')
- down_grad: bfloat16 [26624, 8192], P('tp', 'fsdp')
The draws below stay inside these ranges and needn't reach their ends.
All inputs are finite; a program needn't handle non-finite values.
Results may differ from the reference program's by a relative error of at most 0.023.
Values may be sent and summed in bfloat16 or wider, within the bound.
A program may use at most 192 MiB of HBM per device.

```python
import jax
import jax.numpy as jnp
from jax import lax

D = 8192
FF = 26624
TOK_GROUP = 256
TOKENS = 2048
N_FSDP = 8
N_TP = 16


def raised(drawn, key, source, target, blocks, factor):
    def block_of(axis_at):
        return (jnp.arange(drawn.shape[axis_at]) // (drawn.shape[axis_at] // blocks)).reshape((-1,) + (1,) * (drawn.ndim - 1 - axis_at))

    near = jax.random.permutation(key, blocks)[block_of(target)]
    far = (block_of(target) + blocks // 2) % blocks
    return jnp.where((block_of(source) == near) | (block_of(source) == far), factor * drawn, drawn)


def levels(key, shape, shards, low, high):
    loudness = 1.0
    for position, shards_of in shards:
        draws = jax.random.uniform(jax.random.fold_in(jax.random.fold_in(key, 6), position), (shards_of,), jnp.float32, low / len(shards), high / len(shards))
        loudness = loudness * jnp.repeat(jnp.exp(draws), shape[position] // shards_of).reshape((-1,) + (1,) * (len(shape) - 1 - position))
    return loudness


def centred(stream_key, shape, scale, limit, cuts=(), kind=jnp.bfloat16):
    level = levels(stream_key, shape, cuts, -0.22, 0.18) if cuts else 1.0
    values = jax.random.normal(stream_key, shape, jnp.float32) * scale * level
    return jnp.minimum(jnp.maximum(values, -limit), limit).astype(kind)


def gaussian_with(stream_key, dims, deviation, most, shards, heavy, dtype=jnp.bfloat16):
    entries = deviation * jax.random.normal(stream_key, dims, jnp.float32)
    if shards:
        entries = entries * levels(stream_key, dims, shards, -0.22, 0.18)
    return jnp.clip(raised(entries, jax.random.fold_in(stream_key, 3), *heavy), -most, most).astype(dtype)


def setup_inputs(seed: int = 0) -> dict:
    keys = jax.random.split(jax.random.key(seed), 5)
    return {
        "gate_pre": centred(keys[0], (TOKENS, FF), 1.5, 9.0, ((0, 8), (1, 16))),
        "up_pre": gaussian_with(keys[1], (TOKENS, FF), 1.0, 6.0, ((0, 8), (1, 16)), (1, 0, 16, 2.0)),
        "down_weight": centred(keys[2], (FF, D), FF ** -0.5, 0.0390625, ((0, 16), (1, 8))),
        "out_grad": gaussian_with(keys[3], (TOKENS, D), 0.25, 6.0, ((0, 128),), (0, 1, 128, 5.5)),
    }


def rounded(value):
    return lax.optimization_barrier(value.astype(jnp.bfloat16)).astype(jnp.float32)


def reference(gate_pre, up_pre, down_weight, out_grad):
    gate = gate_pre.astype(jnp.float32)
    up_sum = up_pre.astype(jnp.float32)
    sigmoid = jax.nn.sigmoid(gate)
    hidden = (gate * sigmoid * up_sum).astype(jnp.bfloat16)
    block = FF // N_TP

    def add_block(index, total):
        first = (index * block).astype(jnp.int32)
        piece_hidden = lax.dynamic_slice_in_dim(hidden, first, block, 1)
        piece_weight = lax.dynamic_slice_in_dim(down_weight, first, block, 0)
        return total + rounded(jnp.dot(piece_hidden, piece_weight, preferred_element_type=jnp.float32))

    layer_total = lax.fori_loop(jnp.int32(0), jnp.int32(N_TP), add_block,
                                jnp.zeros((TOKENS, D), jnp.float32))
    hidden_grad = jnp.dot(out_grad, down_weight.T, preferred_element_type=jnp.float32)
    gate_delta = (hidden_grad * up_sum * sigmoid * (1.0 + gate * (1.0 - sigmoid))).astype(jnp.bfloat16)
    up_delta = (hidden_grad * gate * sigmoid).astype(jnp.bfloat16)

    def add_group(index, total):
        first = (index * TOK_GROUP).astype(jnp.int32)
        piece_hidden = lax.dynamic_slice_in_dim(hidden, first, TOK_GROUP, 0)
        piece_grad = lax.dynamic_slice_in_dim(out_grad, first, TOK_GROUP, 0)
        return total + rounded(jnp.dot(piece_hidden.T, piece_grad, preferred_element_type=jnp.float32))

    down_total = lax.fori_loop(jnp.int32(0), jnp.int32(N_FSDP), add_group,
                               jnp.zeros((FF, D), jnp.float32))
    return (layer_total.astype(jnp.bfloat16), gate_delta, up_delta, down_total.astype(jnp.bfloat16))
```

```python
import jax
import jax.numpy as jnp
from jax import lax
from jax.sharding import PartitionSpec as P


def dot(left, right, dims):
    return lax.dot_general(left, right, (dims, ((), ())), preferred_element_type=jnp.float32)


def body(gate_pre, up_pre, down_weight, out_grad):
    tokens, units = gate_pre.shape
    rows, features = out_grad.shape
    groups = lax.axis_size("fsdp")
    gate = gate_pre.astype(jnp.float32)
    up_sum = up_pre.astype(jnp.float32)
    sigmoid = jax.nn.sigmoid(gate)
    hidden = (gate * sigmoid * up_sum).astype(jnp.bfloat16)
    all_hidden = lax.all_gather(hidden, "fsdp", axis=0, tiled=True)
    grads = lax.all_to_all(out_grad, "fsdp", split_axis=1, concat_axis=0, tiled=True)
    grads = grads.reshape(groups, rows, features // groups)
    grads = lax.all_gather(grads, "tp", axis=1, tiled=True)
    grads = grads.reshape(groups * tokens, features // groups)
    hidden_grad = dot(grads, down_weight, ((1,), (1,))).astype(jnp.bfloat16)
    hidden_grad = lax.psum_scatter(hidden_grad, "fsdp", scatter_dimension=0, tiled=True).astype(jnp.float32)
    layer = dot(all_hidden, down_weight, ((1,), (0,))).astype(jnp.bfloat16)
    layer = layer.reshape(groups, tokens, features // groups)
    layer = lax.psum_scatter(layer, "tp", scatter_dimension=1, tiled=True)
    layer = layer.reshape(groups * rows, features // groups)
    layer_out = lax.all_to_all(layer, "fsdp", split_axis=0, concat_axis=1, tiled=True)
    down_grad = dot(all_hidden, grads, ((0,), (0,))).astype(jnp.bfloat16)
    gate_delta = (hidden_grad * up_sum * sigmoid * (1.0 + gate * (1.0 - sigmoid))).astype(jnp.bfloat16)
    up_delta = (hidden_grad * gate * sigmoid).astype(jnp.bfloat16)
    return (layer_out, gate_delta, up_delta, down_grad)


def solution(mesh):
    return jax.shard_map(
        body,
        mesh=mesh,
        in_specs=(P("fsdp", "tp"), P("fsdp", "tp"), P("tp", "fsdp"), P(("fsdp", "tp"), None)),
        out_specs=(P(("fsdp", "tp"), None), P("fsdp", "tp"), P("fsdp", "tp"), P("tp", "fsdp")),
        check_vma=False,
    )
```

```python
import jax
import jax.numpy as jnp
from jax import lax
from jax.experimental import pallas as pl
from jax.experimental.pallas import tpu as pltpu
from jax.sharding import PartitionSpec as P

MESH = pl.DeviceIdType.MESH
BF16, F32 = jnp.bfloat16, jnp.float32
NY, NX = 4, 4
GROUPS, SHARES = 8, 16
ROWS, TOK, UNITS, FEAT = 16, 256, 1664, 1024
HALF = TOK // 2
A, B = pl.ds(0, HALF), pl.ds(HALF, HALF)
LO, HI, ALL = pl.ds(0, 4), pl.ds(4, 4), pl.ds(0, 8)
MESSAGES = 80


def loop(count, step):
    def body(i, carry):
        step(i)
        return carry

    lax.fori_loop(0, count, body, 0)


def by_rows(first, count, step):
    loop(count // ROWS, lambda i: step(pl.ds(pl.multiple_of(first + i * ROWS, ROWS), ROWS)))


def kernel(
    gate_in, up_in, weight_in, grads_in,
    layer_ref, gate_delta_ref, up_delta_ref, down_grad_ref,
    gate, up, weight, hidden, grads, gate_factor, up_factor,
    partial, opposite, direct, crossed,
    layer, layer_got, layer_sum, layer_opp, layer_dir, layer_crossed, layer_mine,
    down, gate_delta, up_delta,
    send_sem, recv_sem, local_sem,
):
    f, t = lax.axis_index("fsdp"), lax.axis_index("tp")
    zh, y = f // NY, lax.rem(f, NY)
    x, zl, core = t // 4, lax.rem(t // 2, 2), lax.rem(t, 2)

    def group(k, dy):
        return lax.rem(zh + k, 2) * NY + lax.rem(y + dy + NY, NY)

    def share(k, dx):
        return lax.rem(x + dx + NX, NX) * 4 + lax.rem(zl + k, 2) * 2 + core

    y_next, y_prev, z_other = (group(0, 1), t), (group(0, -1), t), (group(1, 0), t)
    x_next, x_prev, z_near = (f, share(0, 1)), (f, share(0, -1)), (f, share(1, 0))
    c_other = (f, t + 1 - 2 * core)

    used = [0]

    def message(src, dst, device):
        i = used[0]
        used[0] += 1
        return pltpu.make_async_remote_copy(
            src, dst, send_sem.at[i], recv_sem.at[i], device_id=device, device_id_type=MESH
        )

    def same(ref, device):
        return message(ref, ref, device)

    h = {}
    for k in (0, 1):
        mine, prev, next_ = group(k, 0), group(k, -1), group(k, 1)
        h[k, "p", "A"] = same(hidden.at[mine, A], y_next)
        h[k, "m", "A"] = same(hidden.at[mine, A], y_prev)
        h[k, "p", "B"] = same(hidden.at[mine, B], y_next)
        h[k, "m", "B"] = same(hidden.at[mine, B], y_prev)
        h[k, "p", "F"] = same(hidden.at[prev, A], y_next)
        h[k, "m", "F"] = same(hidden.at[next_, B], y_prev)
    hz = {"A": same(hidden.at[f, A], z_other), "B": same(hidden.at[f, B], z_other)}

    def features(i):
        return pl.ds(pl.multiple_of(i * FEAT, FEAT), FEAT)

    def rows_of(i):
        return pl.ds(pl.multiple_of(i * ROWS, ROWS), ROWS)

    def block(i, groups=ALL):
        return grads.at[groups, rows_of(i)]

    ga = []
    for d in range(1, GROUPS):
        to = lax.rem(f + d, GROUPS)
        ga.append(message(grads_in.at[:, features(to)], grads.at[f, rows_of(t)], (to, t)))
    gz = same(block(t), z_near)
    gx, gc = {}, {}
    for k in (0, 1):
        gx[k, "p"] = same(block(share(k, 0)), x_next)
        gx[k, "m"] = same(block(share(k, 0)), x_prev)
        gx[k, "pF"] = same(block(share(k, -1), LO), x_next)
        gx[k, "mF"] = same(block(share(k, 1), HI), x_prev)
        for dx in (0, -1, 1, 2):
            gc[k, dx] = same(block(share(k, dx)), c_other)

    r = {}
    for k in (0, 1):
        far, next_, prev = group(k, 2), group(k, 1), group(k, -1)
        r[k, "p", "O"] = message(partial.at[far, A], opposite.at[k, 0], y_next)
        r[k, "m", "O"] = message(partial.at[far, B], opposite.at[k, 1], y_prev)
        r[k, "p", "I"] = message(partial.at[next_, B], direct.at[k, 0, B], y_next)
        r[k, "m", "I"] = message(partial.at[prev, A], direct.at[k, 1, A], y_prev)
        r[k, "p", "D"] = message(partial.at[next_, A], direct.at[k, 0, A], y_next)
        r[k, "m", "D"] = message(partial.at[prev, B], direct.at[k, 1, B], y_prev)
    rz = {s: message(partial.at[group(1, 0), rows], crossed.at[rows], z_other) for s, rows in (("A", A), ("B", B))}

    core_first = used[0]
    used[0] += GROUPS

    def lc(g):
        return pltpu.make_async_remote_copy(
            layer.at[g, :, :, 1 - core], layer_got.at[g], send_sem.at[core_first + g], recv_sem.at[core_first + g],
            device_id=c_other, device_id_type=MESH,
        )

    def chunk(k, dx, groups=ALL):
        return layer_sum.at[groups, lax.rem(x + dx + NX, NX), lax.rem(zl + k, 2)]

    xr = {}
    for k in (0, 1):
        xr[k, "p", "O"] = message(chunk(k, 2, LO), layer_opp.at[k, 0], x_next)
        xr[k, "m", "O"] = message(chunk(k, 2, HI), layer_opp.at[k, 1], x_prev)
        xr[k, "p", "I"] = message(chunk(k, 1, HI), layer_dir.at[k, 0, HI], x_next)
        xr[k, "m", "I"] = message(chunk(k, -1, LO), layer_dir.at[k, 1, LO], x_prev)
        xr[k, "p", "D"] = message(chunk(k, 1, LO), layer_dir.at[k, 0, LO], x_next)
        xr[k, "m", "D"] = message(chunk(k, -1, HI), layer_dir.at[k, 1, HI], x_prev)
    lz = message(chunk(1, 0), layer_crossed, z_near)
    lo = []
    for d in range(1, GROUPS):
        to = lax.rem(f + d, GROUPS)
        lo.append(message(layer_mine.at[to], layer_ref.at[:, features(f)], (to, t)))
    assert used[0] == MESSAGES

    def start(*copies):
        for copy in copies:
            copy.start()

    def got(*copies):
        for copy in copies:
            copy.wait_recv()

    load_gate = pltpu.make_async_copy(gate_in, gate, local_sem.at[0])
    load_up = pltpu.make_async_copy(up_in, up, local_sem.at[1])
    load_weight = pltpu.make_async_copy(weight_in, weight, local_sem.at[2])
    load_grads = pltpu.make_async_copy(grads_in.at[:, features(f)], grads.at[f, rows_of(t)], local_sem.at[3])
    start(load_gate, load_up, load_grads, load_weight)

    barrier = pltpu.get_barrier_semaphore()
    peers = [(lax.rem(f + d, GROUPS), t) for d in range(1, GROUPS)] + [x_next, x_prev, z_near, c_other]
    for peer in peers:
        pl.semaphore_signal(barrier, inc=1, device_id=peer, device_id_type=MESH)
    pl.semaphore_wait(barrier, len(peers))

    start(*ga)

    def activation(rows):
        value = gate[rows].astype(F32)
        hidden[f, rows] = (value * jax.nn.sigmoid(value) * up[rows].astype(F32)).astype(BF16)

    load_gate.wait()
    load_up.wait()
    by_rows(0, HALF, activation)
    start(h[0, "p", "A"], h[0, "m", "A"], hz["A"])
    by_rows(HALF, HALF, activation)
    start(h[0, "p", "B"], h[0, "m", "B"], hz["B"])

    load_grads.wait()
    got(*ga)
    start(gz, gx[0, "p"], gx[0, "m"], gc[0, 0])

    def factors(rows):
        value = gate[rows].astype(F32)
        sigmoid = jax.nn.sigmoid(value)
        gate_factor[rows] = up[rows].astype(F32) * sigmoid * (1.0 + value * (1.0 - sigmoid))
        up_factor[rows] = value * sigmoid

    by_rows(0, TOK, factors)

    got(h[0, "p", "A"])
    start(h[0, "p", "F"])
    got(hz["A"])
    start(h[1, "p", "A"], h[1, "m", "A"])
    got(gz)
    start(gx[1, "p"], gx[1, "m"], gc[1, 0])
    got(gx[0, "p"], gx[0, "m"])
    start(gx[0, "pF"], gx[0, "mF"], gc[0, -1], gc[0, 1])
    got(h[0, "m", "A"], h[0, "m", "B"])
    start(h[0, "m", "F"])
    got(hz["B"])
    start(h[1, "p", "B"], h[1, "m", "B"])
    got(gx[1, "p"], gx[1, "m"])
    start(gx[1, "pF"], gx[1, "mF"], gc[1, -1], gc[1, 1])
    got(gx[0, "pF"], gx[0, "mF"])
    start(gc[0, 2])
    load_weight.wait()
    got(gx[1, "pF"], gx[1, "mF"])
    start(gc[1, 2])
    got(*gc.values())

    def hidden_grad(i):
        k, step = 1 - lax.rem(i, 2), i // 2
        g = lax.rem(zh + k, 2) * NY + lax.rem(y + jnp.where(step == 0, 2, jnp.where(step == 1, 1, jnp.where(step == 2, 3, 0))), NY)
        partial[g] = lax.dot_general(
            grads[g], weight[...], (((1,), (1,)), ((), ())), preferred_element_type=F32
        ).astype(BF16)

        @pl.when(i == 1)
        def _():
            start(r[1, "p", "O"], r[1, "m", "O"], r[0, "p", "O"], r[0, "m", "O"])

        @pl.when(i == 4)
        def _():
            got(h[1, "p", "A"])
            start(h[1, "p", "F"])

    loop(8, hidden_grad)
    got(h[1, "m", "A"], h[1, "m", "B"])
    start(h[1, "m", "F"])
    start(r[1, "p", "I"], r[1, "m", "I"])

    def add_into(target, k, side, rows_first):
        def step(rows):
            source = pl.ds(pl.multiple_of(rows.start - rows_first, ROWS), ROWS)
            partial[target, rows] = (
                partial[target, rows].astype(F32) + opposite[k, side, source].astype(F32)
            ).astype(BF16)

        by_rows(rows_first, HALF, step)

    def pass_on(k):
        got(r[k, "p", "O"])
        add_into(group(k, 1), k, 0, 0)
        start(r[k, "p", "D"])
        got(r[k, "m", "O"])
        add_into(group(k, -1), k, 1, HALF)
        start(r[k, "m", "D"])

    pass_on(1)
    start(r[0, "p", "I"], r[0, "m", "I"])

    got(h[0, "p", "B"], h[0, "p", "F"], h[0, "m", "F"])
    got(h[1, "p", "B"], h[1, "p", "F"], h[1, "m", "F"])

    def layer_partial(g):
        value = jnp.dot(hidden[g], weight[...], preferred_element_type=F32).astype(BF16)
        layer[g] = value.reshape(4, 2, 2, ROWS, FEAT)
        lc(g).start()

    loop(8, layer_partial)
    pass_on(0)

    def layer_add(g):
        lc(g).wait_recv()
        for at in range(4):
            layer_sum[g, at] = (layer[g, at, :, core].astype(F32) + layer_got[g, at].astype(F32)).astype(BF16)

    loop(8, layer_add)
    start(xr[1, "p", "O"], xr[1, "m", "O"], xr[0, "p", "O"], xr[0, "m", "O"])
    start(xr[1, "p", "I"], xr[1, "m", "I"], xr[0, "p", "I"], xr[0, "m", "I"])

    def layer_pass_on(k):
        for side, dx, first, name in ((0, 1, 0, "p"), (1, -1, 4, "m")):
            got(xr[k, name, "O"])
            at, z = lax.rem(x + dx + NX, NX), lax.rem(zl + k, 2)

            def step(i, side=side, first=first, at=at, z=z):
                layer_sum[first + i, at, z] = (
                    layer_sum[first + i, at, z].astype(F32) + layer_opp[k, side, i].astype(F32)
                ).astype(BF16)

            loop(4, step)
            start(xr[k, name, "D"])

    def down_strip(i):
        units = pl.ds(pl.multiple_of(i * 128, 128), 128)
        total = jnp.zeros((128, FEAT), F32)
        for g in range(GROUPS):
            total += lax.dot_general(
                hidden[g, :, units], grads[g], (((0,), (0,)), ((), ())), preferred_element_type=F32
            )
        down[units] = total.astype(BF16)

        @pl.when(i == 2)
        def _():
            layer_pass_on(1)
            layer_pass_on(0)

        @pl.when(i == 9)
        def _():
            got(xr[1, "p", "I"], xr[1, "m", "I"], xr[1, "p", "D"], xr[1, "m", "D"])

            def step(g):
                z = 1 - zl
                layer_sum[g, x, z] = (
                    layer_sum[g, x, z].astype(F32) + layer_dir[1, 0, g].astype(F32) + layer_dir[1, 1, g].astype(F32)
                ).astype(BF16)

            loop(8, step)
            start(lz)

    loop(13, down_strip)
    store_down = pltpu.make_async_copy(down, down_grad_ref, local_sem.at[4])
    store_down.start()

    mine = group(1, 0)
    for s, first, names in (("B", HALF, (("p", "I"), ("m", "D"))), ("A", 0, (("p", "D"), ("m", "I")))):
        for side, kind in names:
            got(r[1, side, kind])

        def step(rows):
            partial[mine, rows] = (
                partial[mine, rows].astype(F32) + direct[1, 0, rows].astype(F32) + direct[1, 1, rows].astype(F32)
            ).astype(BF16)

        by_rows(first, HALF, step)
        start(rz[s])

    got(xr[0, "p", "I"], xr[0, "m", "I"], xr[0, "p", "D"], xr[0, "m", "D"], lz)

    def layer_final(g):
        layer_mine[g] = (
            layer_sum[g, x, zl].astype(F32) + layer_dir[0, 0, g].astype(F32)
            + layer_dir[0, 1, g].astype(F32) + layer_crossed[g].astype(F32)
        ).astype(BF16)

    loop(8, layer_final)
    start(*lo)
    store_layer = pltpu.make_async_copy(layer_mine.at[f], layer_ref.at[:, features(f)], local_sem.at[5])
    store_layer.start()

    stores = []
    for s, first, names in (("B", HALF, (("p", "I"), ("m", "D"))), ("A", 0, (("p", "D"), ("m", "I")))):
        for side, kind in names:
            got(r[0, side, kind])
        got(rz[s])

        def step(rows):
            total = (
                partial[f, rows].astype(F32) + direct[0, 0, rows].astype(F32)
                + direct[0, 1, rows].astype(F32) + crossed[rows].astype(F32)
            )
            gate_delta[rows] = (total * gate_factor[rows]).astype(BF16)
            up_delta[rows] = (total * up_factor[rows]).astype(BF16)

        by_rows(first, HALF, step)
        rows = pl.ds(first, HALF)
        stores.append(pltpu.make_async_copy(gate_delta.at[rows], gate_delta_ref.at[rows], local_sem.at[6 + len(stores)]))
        stores.append(pltpu.make_async_copy(up_delta.at[rows], up_delta_ref.at[rows], local_sem.at[6 + len(stores)]))
        start(*stores[-2:])

    got(*lo)
    for copy in [*h.values(), *hz.values(), *ga, gz, *gx.values(), *gc.values(), *r.values(), *rz.values(), *xr.values(), lz, *lo]:
        copy.wait_send()
    loop(GROUPS, lambda g: lc(g).wait_send())
    for copy in [store_down, store_layer, *stores]:
        copy.wait()


def body(gate_pre, up_pre, down_weight, out_grad):
    anywhere = pl.BlockSpec(memory_space=pl.ANY)
    v = pltpu.VMEM
    return pl.pallas_call(
        kernel,
        name="feed_forward",
        out_shape=(
            jax.ShapeDtypeStruct(out_grad.shape, BF16),
            jax.ShapeDtypeStruct(gate_pre.shape, BF16),
            jax.ShapeDtypeStruct(up_pre.shape, BF16),
            jax.ShapeDtypeStruct(down_weight.shape, BF16),
        ),
        in_specs=[anywhere] * 4,
        out_specs=[anywhere] * 4,
        scratch_shapes=[
            v((TOK, UNITS), BF16),
            v((TOK, UNITS), BF16),
            v((UNITS, FEAT), BF16),
            v((GROUPS, TOK, UNITS), BF16),
            v((GROUPS, TOK, FEAT), BF16),
            v((TOK, UNITS), F32),
            v((TOK, UNITS), F32),
            v((GROUPS, TOK, UNITS), BF16),
            v((2, 2, HALF, UNITS), BF16),
            v((2, 2, TOK, UNITS), BF16),
            v((TOK, UNITS), BF16),
            v((GROUPS, 4, 2, 2, ROWS, FEAT), BF16),
            v((GROUPS, 4, 2, ROWS, FEAT), BF16),
            v((GROUPS, 4, 2, ROWS, FEAT), BF16),
            v((2, 2, 4, ROWS, FEAT), BF16),
            v((2, 2, GROUPS, ROWS, FEAT), BF16),
            v((GROUPS, ROWS, FEAT), BF16),
            v((GROUPS, ROWS, FEAT), BF16),
            v((UNITS, FEAT), BF16),
            v((TOK, UNITS), BF16),
            v((TOK, UNITS), BF16),
            pltpu.SemaphoreType.DMA((MESSAGES,)),
            pltpu.SemaphoreType.DMA((MESSAGES,)),
            pltpu.SemaphoreType.DMA((10,)),
        ],
        compiler_params=pltpu.CompilerParams(
            collective_id=0, has_side_effects=True, vmem_limit_bytes=62 << 20
        ),
        cost_estimate=pl.CostEstimate(flops=21_000_000_000, bytes_accessed=12_000_000, transcendentals=400_000),
    )(gate_pre, up_pre, down_weight, out_grad)


def solution(mesh):
    return jax.shard_map(
        body,
        mesh=mesh,
        in_specs=(P("fsdp", "tp"), P("fsdp", "tp"), P("tp", "fsdp"), P(("fsdp", "tp"), None)),
        out_specs=(P(("fsdp", "tp"), None), P("fsdp", "tp"), P("fsdp", "tp"), P("tp", "fsdp")),
        check_vma=False,
    )
```

```python
import jax
import jax.numpy as jnp
from jax import lax
from jax.experimental import pallas as pl
from jax.experimental.pallas import tpu as pltpu
from jax.sharding import PartitionSpec as P

MESH = pl.DeviceIdType.MESH
BF16, F32 = jnp.bfloat16, jnp.float32
NY, NX = 4, 4
GROUPS, SHARES = 8, 16
ROWS, TOK, UNITS, FEAT = 16, 256, 1664, 1024
RING = 96
R, Z = (0, RING), (RING, TOK - RING)
LO, HI, ALL = pl.ds(0, 4), pl.ds(4, 4), pl.ds(0, 8)
CLASSES = (0, 1)
MESSAGES = 106


def whole(part):
    return pl.ds(*part)


def first(part):
    return pl.ds(part[0], part[1] // 2)


def second(part):
    return pl.ds(part[0] + part[1] // 2, part[1] // 2)


def loop(count, step):
    def body(i, carry):
        step(i)
        return carry

    lax.fori_loop(0, count, body, 0)


def by_rows(first, count, step):
    loop(count // ROWS, lambda i: step(pl.ds(pl.multiple_of(first + i * ROWS, ROWS), ROWS)))


def kernel(
    gate_in, up_in, weight_in, grads_in,
    layer_ref, gate_delta_ref, up_delta_ref, down_grad_ref,
    gate, up, weight, hidden, grads, gate_factor, up_factor,
    partial, opposite, direct, crossed, crossed_ring,
    layer, layer_got, layer_sum, layer_opp, layer_dir, layer_crossed, layer_mine,
    down, gate_delta, up_delta,
    send_sem, recv_sem, local_sem,
):
    f, t = lax.axis_index("fsdp"), lax.axis_index("tp")
    zh, y = f // NY, lax.rem(f, NY)
    x, zl, core = t // 4, lax.rem(t // 2, 2), lax.rem(t, 2)

    def group(k, dy):
        return lax.rem(zh + k, 2) * NY + lax.rem(y + dy + NY, NY)

    def share(k, dx):
        return lax.rem(x + dx + NX, NX) * 4 + lax.rem(zl + k, 2) * 2 + core

    y_next, y_prev, z_other = (group(0, 1), t), (group(0, -1), t), (group(1, 0), t)
    x_next, x_prev, z_near = (f, share(0, 1)), (f, share(0, -1)), (f, share(1, 0))
    c_other = (f, t + 1 - 2 * core)

    used = [0]

    def message(src, dst, device):
        i = used[0]
        used[0] += 1
        return pltpu.make_async_remote_copy(
            src, dst, send_sem.at[i], recv_sem.at[i], device_id=device, device_id_type=MESH
        )

    def same(ref, device):
        return message(ref, ref, device)

    h, hz = {}, {}
    for k, part in ((0, Z), (0, R), (1, Z)):
        mine, prev, next_ = group(k, 0), group(k, -1), group(k, 1)
        h[k, part, "p"] = same(hidden.at[mine, whole(part)], y_next)
        h[k, part, "m"] = same(hidden.at[mine, whole(part)], y_prev)
        h[k, part, "pF"] = same(hidden.at[prev, first(part)], y_next)
        h[k, part, "mF"] = same(hidden.at[next_, second(part)], y_prev)
    hz["Z"] = same(hidden.at[f, whole(Z)], z_other)
    for dy in (0, 1, -1, 2):
        hz[dy] = same(hidden.at[group(0, dy), whole(R)], z_other)

    def features(i):
        return pl.ds(pl.multiple_of(i * FEAT, FEAT), FEAT)

    def rows_of(i):
        return pl.ds(pl.multiple_of(i * ROWS, ROWS), ROWS)

    def block(i, groups=ALL):
        return grads.at[groups, rows_of(i)]

    ga = []
    for d in range(1, GROUPS):
        to = lax.rem(f + d, GROUPS)
        ga.append(message(grads_in.at[:, features(to)], grads.at[f, rows_of(t)], (to, t)))
    gz = same(block(t), z_near)
    gx, gc = {}, {}
    for k in (0, 1):
        gx[k, "p"] = same(block(share(k, 0)), x_next)
        gx[k, "m"] = same(block(share(k, 0)), x_prev)
        gx[k, "pF"] = same(block(share(k, -1), LO), x_next)
        gx[k, "mF"] = same(block(share(k, 1), HI), x_prev)
        for dx in (0, -1, 1, 2):
            gc[k, dx] = same(block(share(k, dx)), c_other)

    r = {}
    for n, (k, part) in enumerate(((1, Z), (0, Z), (0, R))):
        far, next_, prev = group(k, 2), group(k, 1), group(k, -1)
        half = pl.ds(0, part[1] // 2)
        r[k, part, "pO"] = message(partial.at[far, first(part)], opposite.at[n, 0, half], y_next)
        r[k, part, "mO"] = message(partial.at[far, second(part)], opposite.at[n, 1, half], y_prev)
        r[k, part, "pI"] = message(partial.at[next_, second(part)], direct.at[k, 0, second(part)], y_next)
        r[k, part, "mI"] = message(partial.at[prev, first(part)], direct.at[k, 1, first(part)], y_prev)
        r[k, part, "pD"] = message(partial.at[next_, first(part)], direct.at[k, 0, first(part)], y_next)
        r[k, part, "mD"] = message(partial.at[prev, second(part)], direct.at[k, 1, second(part)], y_prev)
    rz = [message(partial.at[group(1, 0), rows], crossed.at[rows], z_other) for rows in (first(Z), second(Z))]
    rr = {dy: message(partial.at[group(1, dy), whole(R)], crossed_ring.at[dy % NY], z_other) for dy in (2, 1, -1, 0)}

    core_first = used[0]
    used[0] += GROUPS

    def lc(g):
        return pltpu.make_async_remote_copy(
            layer.at[g, :, :, 1 - core], layer_got.at[g], send_sem.at[core_first + g], recv_sem.at[core_first + g],
            device_id=c_other, device_id_type=MESH,
        )

    def chunk(k, dx, groups=ALL):
        return layer_sum.at[groups, lax.rem(x + dx + NX, NX), lax.rem(zl + k, 2)]

    def of_class(batch, at=0, count=4):
        return pl.ds(lax.rem(zh + batch, 2) * NY + at, count)

    xr, lz = {}, {}
    for b in CLASSES:
        near, far = of_class(b, 0, 2), of_class(b, 2, 2)
        for k in (0, 1):
            xr[b, k, "pO"] = message(chunk(k, 2, near), layer_opp.at[b, k, 0], x_next)
            xr[b, k, "mO"] = message(chunk(k, 2, far), layer_opp.at[b, k, 1], x_prev)
            xr[b, k, "pI"] = message(chunk(k, 1, far), layer_dir.at[k, 0, far], x_next)
            xr[b, k, "mI"] = message(chunk(k, -1, near), layer_dir.at[k, 1, near], x_prev)
            xr[b, k, "pD"] = message(chunk(k, 1, near), layer_dir.at[k, 0, near], x_next)
            xr[b, k, "mD"] = message(chunk(k, -1, far), layer_dir.at[k, 1, far], x_prev)
        lz[b] = message(chunk(1, 0, of_class(b)), layer_crossed.at[of_class(b)], z_near)
    lo = {}
    for d in range(1, GROUPS):
        to = group(d // NY, d % NY)
        lo[d] = message(layer_mine.at[to], layer_ref.at[:, features(f)], (to, t))
    assert used[0] == MESSAGES

    def start(*copies):
        for copy in copies:
            copy.start()

    def got(*copies):
        for copy in copies:
            copy.wait_recv()

    load_gate = pltpu.make_async_copy(gate_in, gate, local_sem.at[0])
    load_up = pltpu.make_async_copy(up_in, up, local_sem.at[1])
    load_weight = pltpu.make_async_copy(weight_in, weight, local_sem.at[2])
    load_grads = pltpu.make_async_copy(grads_in.at[:, features(f)], grads.at[f, rows_of(t)], local_sem.at[3])
    start(load_gate, load_up, load_grads, load_weight)

    barrier = pltpu.get_barrier_semaphore()
    peers = [(lax.rem(f + d, GROUPS), t) for d in range(1, GROUPS)] + [x_next, x_prev, z_near, c_other]
    for peer in peers:
        pl.semaphore_signal(barrier, inc=1, device_id=peer, device_id_type=MESH)
    pl.semaphore_wait(barrier, len(peers))

    start(*ga)

    def activation(rows):
        value = gate[rows].astype(F32)
        hidden[f, rows] = (value * jax.nn.sigmoid(value) * up[rows].astype(F32)).astype(BF16)

    load_gate.wait()
    load_up.wait()
    by_rows(*Z, activation)
    start(hz["Z"], h[0, Z, "p"], h[0, Z, "m"])
    by_rows(*R, activation)
    start(h[0, R, "p"], h[0, R, "m"])

    load_grads.wait()
    got(*ga)
    start(gz, gx[0, "p"], gx[0, "m"], gc[0, 0])

    def factors(rows):
        value = gate[rows].astype(F32)
        sigmoid = jax.nn.sigmoid(value)
        gate_factor[rows] = up[rows].astype(F32) * sigmoid * (1.0 + value * (1.0 - sigmoid))
        up_factor[rows] = value * sigmoid

    def layer_partial(g):
        value = jnp.dot(hidden[g], weight[...], preferred_element_type=F32).astype(BF16)
        layer[g] = value.reshape(4, 2, 2, ROWS, FEAT)
        lc(g).start()

    by_rows(0, TOK, factors)
    load_weight.wait()

    got(gx[0, "p"], gx[0, "m"])
    start(gx[0, "pF"], gx[0, "mF"], gc[0, -1], gc[0, 1])
    got(h[0, Z, "p"], h[0, Z, "m"])
    start(h[0, Z, "pF"], h[0, Z, "mF"])
    got(gz)
    start(gx[1, "p"], gx[1, "m"], gc[1, 0])
    got(hz["Z"])
    start(h[1, Z, "p"], h[1, Z, "m"], hz[0])
    got(gx[0, "pF"], gx[0, "mF"])
    start(gc[0, 2])
    got(h[0, R, "p"], h[0, R, "m"])
    start(h[0, R, "pF"], h[0, R, "mF"], hz[1], hz[-1])

    def layer_early(i):
        layer_partial(lax.rem(zh, 2) * NY + lax.rem(y + jnp.where(i == 0, 0, jnp.where(i == 1, 1, jnp.where(i == 2, 3, 2))), NY))

        @pl.when(i == 2)
        def _():
            got(gx[1, "p"], gx[1, "m"])
            start(gx[1, "pF"], gx[1, "mF"], gc[1, -1], gc[1, 1])
            got(h[0, R, "pF"], h[0, R, "mF"])
            start(hz[2])
            got(h[0, Z, "pF"], h[0, Z, "mF"])

    loop(4, layer_early)
    got(gx[1, "pF"], gx[1, "mF"])
    start(gc[1, 2])
    got(*gc.values())

    def layer_add(b):
        def step(i):
            g = lax.rem(zh + b, 2) * NY + i
            lc(g).wait_recv()
            for at in range(4):
                layer_sum[g, at] = (layer[g, at, :, core].astype(F32) + layer_got[g, at].astype(F32)).astype(BF16)

        loop(4, step)
        start(*[xr[b, k, name] for name in ("pO", "mO", "pI", "mI") for k in (1, 0)])

    def layer_pass_on(b):
        for k in (1, 0):
            for side, dx, at_first, name in ((0, 1, 0, "p"), (1, -1, 2, "m")):
                got(xr[b, k, name + "O"])
                at, z = lax.rem(x + dx + NX, NX), lax.rem(zl + k, 2)
                at_first = lax.rem(zh + b, 2) * NY + at_first

                def step(i, side=side, at_first=at_first, at=at, z=z, k=k):
                    layer_sum[at_first + i, at, z] = (
                        layer_sum[at_first + i, at, z].astype(F32) + layer_opp[b, k, side, i].astype(F32)
                    ).astype(BF16)

                loop(2, step)
                start(xr[b, k, name + "D"])

    def layer_cross(b):
        got(*[xr[b, 1, name] for name in ("pI", "mI", "pD", "mD")])

        def step(i):
            g, z = lax.rem(zh + b, 2) * NY + i, 1 - zl
            layer_sum[g, x, z] = (
                layer_sum[g, x, z].astype(F32) + layer_dir[1, 0, g].astype(F32) + layer_dir[1, 1, g].astype(F32)
            ).astype(BF16)

        loop(4, step)
        start(lz[b])

    def layer_finish(b):
        got(*[xr[b, 0, name] for name in ("pI", "mI", "pD", "mD")], lz[b])

        def step(i):
            g = lax.rem(zh + b, 2) * NY + i
            layer_mine[g] = (
                layer_sum[g, x, zl].astype(F32) + layer_dir[0, 0, g].astype(F32)
                + layer_dir[0, 1, g].astype(F32) + layer_crossed[g].astype(F32)
            ).astype(BF16)

        loop(4, step)
        start(*[lo[d] for d in lo if d // NY == b])

    def hidden_grad(i):
        k, at = 1 - i // 4, lax.rem(i, 4)
        dy = jnp.where(at == 0, 2, jnp.where(at == 1, 1, jnp.where(at == 2, 3, 0)))
        g = lax.rem(zh + k, 2) * NY + lax.rem(y + dy, NY)
        partial[g] = lax.dot_general(
            grads[g], weight[...], (((1,), (1,)), ((), ())), preferred_element_type=F32
        ).astype(BF16)

        @pl.when(i == 0)
        def _():
            start(r[1, Z, "pO"], r[1, Z, "mO"], rr[2])

        @pl.when(i == 1)
        def _():
            start(r[1, Z, "pI"], rr[1])

        @pl.when(i == 2)
        def _():
            start(r[1, Z, "mI"], rr[-1])

        @pl.when(i == 3)
        def _():
            start(rr[0])

        @pl.when(i == 4)
        def _():
            layer_add(0)

    loop(8, hidden_grad)
    got(h[1, Z, "p"], h[1, Z, "m"])
    start(h[1, Z, "pF"], h[1, Z, "mF"])

    def add_into(target, source, at, count):
        def step(i):
            rows = pl.ds(pl.multiple_of(at + i * ROWS, ROWS), ROWS)
            other = pl.ds(pl.multiple_of(i * ROWS, ROWS), ROWS)
            partial[target, rows] = (partial[target, rows].astype(F32) + source[other].astype(F32)).astype(BF16)

        loop(count // ROWS, step)

    def pass_on(n, k, part):
        half = part[1] // 2
        got(r[k, part, "pO"])
        add_into(group(k, 1), opposite.at[n, 0], part[0], half)
        start(r[k, part, "pD"])
        got(r[k, part, "mO"])
        add_into(group(k, -1), opposite.at[n, 1], part[0] + half, half)
        start(r[k, part, "mD"])

    start(r[0, Z, "pO"], r[0, Z, "mO"], r[0, Z, "pI"], r[0, Z, "mI"])
    layer_pass_on(0)
    pass_on(0, 1, Z)

    got(h[1, Z, "pF"], h[1, Z, "mF"], *[hz[dy] for dy in (0, 1, -1, 2)])
    loop(4, lambda i: layer_partial(lax.rem(zh + 1, 2) * NY + i))
    layer_cross(0)
    pass_on(1, 0, Z)
    layer_add(1)

    def ring_add(dy):
        got(rr[dy])
        add_into(group(0, dy), crossed_ring.at[dy % NY], R[0], R[1])

    def cross():
        mine = group(1, 0)
        for copy, rows, names in ((rz[0], first(Z), ("pD", "mI")), (rz[1], second(Z), ("pI", "mD"))):
            got(*[r[1, Z, name] for name in names])

            def step(at):
                partial[mine, at] = (
                    partial[mine, at].astype(F32) + direct[1, 0, at].astype(F32) + direct[1, 1, at].astype(F32)
                ).astype(BF16)

            by_rows(rows.start, rows.size, step)
            start(copy)

    def down_strip(i):
        units = pl.ds(pl.multiple_of(i * 128, 128), 128)
        total = jnp.zeros((128, FEAT), F32)
        for g in range(GROUPS):
            total += lax.dot_general(
                hidden[g, :, units], grads[g], (((0,), (0,)), ((), ())), preferred_element_type=F32
            )
        down[units] = total.astype(BF16)

        @pl.when(i == 1)
        def _():
            ring_add(2)
            start(r[0, R, "pO"], r[0, R, "mO"])

        @pl.when(i == 3)
        def _():
            layer_pass_on(1)

        @pl.when(i == 5)
        def _():
            cross()
            ring_add(1)
            start(r[0, R, "pI"])
            ring_add(-1)
            start(r[0, R, "mI"])

        @pl.when(i == 7)
        def _():
            layer_finish(0)

        @pl.when(i == 9)
        def _():
            layer_cross(1)

        @pl.when(i == 11)
        def _():
            pass_on(2, 0, R)

    loop(13, down_strip)
    store_down = pltpu.make_async_copy(down, down_grad_ref, local_sem.at[4])
    store_down.start()

    layer_finish(1)
    store_layer = pltpu.make_async_copy(layer_mine.at[f], layer_ref.at[:, features(f)], local_sem.at[5])
    store_layer.start()

    stores = []
    got(rr[0])

    def finish(part, rows):
        def step(i):
            at = pl.ds(pl.multiple_of(rows.start + i * ROWS, ROWS), ROWS)
            total = partial[f, at].astype(F32) + direct[0, 0, at].astype(F32) + direct[0, 1, at].astype(F32)
            if part is R:
                total += crossed_ring[0, at].astype(F32)
            else:
                total += crossed[at].astype(F32)
            gate_delta[at] = (total * gate_factor[at]).astype(BF16)
            up_delta[at] = (total * up_factor[at]).astype(BF16)

        loop(rows.size // ROWS, step)
        stores.append(pltpu.make_async_copy(gate_delta.at[rows], gate_delta_ref.at[rows], local_sem.at[6 + len(stores)]))
        stores.append(pltpu.make_async_copy(up_delta.at[rows], up_delta_ref.at[rows], local_sem.at[6 + len(stores)]))
        start(*stores[-2:])

    got(*[r[0, Z, name] for name in ("pI", "mI", "pD", "mD")], *rz)
    finish(Z, whole(Z))
    got(*[r[0, R, name] for name in ("pI", "mI", "pD", "mD")])
    finish(R, whole(R))

    got(*lo.values())
    for copy in [*h.values(), *hz.values(), *ga, gz, *gx.values(), *gc.values(), *r.values(), *rz, *rr.values(), *xr.values(), *lz.values(), *lo.values()]:
        copy.wait_send()
    loop(GROUPS, lambda g: lc(g).wait_send())
    for copy in [store_down, store_layer, *stores]:
        copy.wait()


def hand_over(*refs):
    sources, targets, held, load_sem, store_sem = refs[:4], refs[4:8], refs[8:12], refs[12], refs[13]
    parts = [(3, pl.ds(i * UNITS // 4, UNITS // 4)) for i in range(4)] + [(1, pl.ds(0, TOK)), (2, pl.ds(0, TOK)), (0, pl.ds(0, ROWS))]
    loads = [pltpu.make_async_copy(sources[a].at[p], held[a].at[p], load_sem.at[i]) for i, (a, p) in enumerate(parts)]
    stores = [pltpu.make_async_copy(held[a].at[p], targets[a].at[p], store_sem.at[i]) for i, (a, p) in enumerate(parts)]
    for load in loads:
        load.start()
    for load, store in zip(loads, stores):
        load.wait()
        store.start()
    for store in stores:
        store.wait()


def body(gate_pre, up_pre, down_weight, out_grad):
    anywhere = pl.BlockSpec(memory_space=pl.ANY)
    v = pltpu.VMEM
    outs = pl.pallas_call(
        kernel,
        name="feed_forward",
        out_shape=(
            jax.ShapeDtypeStruct(out_grad.shape, BF16),
            jax.ShapeDtypeStruct(gate_pre.shape, BF16),
            jax.ShapeDtypeStruct(up_pre.shape, BF16),
            jax.ShapeDtypeStruct(down_weight.shape, BF16),
        ),
        in_specs=[anywhere] * 4,
        out_specs=[anywhere] * 4,
        scratch_shapes=[
            v((TOK, UNITS), BF16),
            v((TOK, UNITS), BF16),
            v((UNITS, FEAT), BF16),
            v((GROUPS, TOK, UNITS), BF16),
            v((GROUPS, TOK, FEAT), BF16),
            v((TOK, UNITS), F32),
            v((TOK, UNITS), F32),
            v((GROUPS, TOK, UNITS), BF16),
            v((3, 2, Z[1] // 2, UNITS), BF16),
            v((2, 2, TOK, UNITS), BF16),
            v((TOK, UNITS), BF16),
            v((NY, RING, UNITS), BF16),
            v((GROUPS, 4, 2, 2, ROWS, FEAT), BF16),
            v((GROUPS, 4, 2, ROWS, FEAT), BF16),
            v((GROUPS, 4, 2, ROWS, FEAT), BF16),
            v((2, 2, 2, 2, ROWS, FEAT), BF16),
            v((2, 2, GROUPS, ROWS, FEAT), BF16),
            v((GROUPS, ROWS, FEAT), BF16),
            v((GROUPS, ROWS, FEAT), BF16),
            v((UNITS, FEAT), BF16),
            v((TOK, UNITS), BF16),
            v((TOK, UNITS), BF16),
            pltpu.SemaphoreType.DMA((MESSAGES,)),
            pltpu.SemaphoreType.DMA((MESSAGES,)),
            pltpu.SemaphoreType.DMA((10,)),
        ],
        compiler_params=pltpu.CompilerParams(
            collective_id=0, has_side_effects=True, vmem_limit_bytes=62 << 20
        ),
        cost_estimate=pl.CostEstimate(flops=21_000_000_000, bytes_accessed=12_000_000, transcendentals=400_000),
    )(gate_pre, up_pre, down_weight, out_grad)
    return pl.pallas_call(
        hand_over,
        name="hand_over",
        out_shape=tuple(jax.ShapeDtypeStruct(out.shape, BF16) for out in outs),
        in_specs=[anywhere] * 4,
        out_specs=[anywhere] * 4,
        scratch_shapes=[v(out.shape, BF16) for out in outs] + [pltpu.SemaphoreType.DMA((7,))] * 2,
        cost_estimate=pl.CostEstimate(flops=0, bytes_accessed=12_000_000, transcendentals=0),
    )(*outs)


def solution(mesh):
    return jax.shard_map(
        body,
        mesh=mesh,
        in_specs=(P("fsdp", "tp"), P("fsdp", "tp"), P("tp", "fsdp"), P(("fsdp", "tp"), None)),
        out_specs=(P(("fsdp", "tp"), None), P("fsdp", "tp"), P("fsdp", "tp"), P("tp", "fsdp")),
        check_vma=False,
    )
```

```python
import jax
import jax.numpy as jnp
from jax import lax
from jax.experimental import pallas as pl
from jax.experimental.pallas import tpu as pltpu
from jax.sharding import PartitionSpec as P

MESH = pl.DeviceIdType.MESH
BF16, F32 = jnp.bfloat16, jnp.float32
NY, NX = 4, 4
GROUPS, SHARES = 8, 16
ROWS, TOK, UNITS, FEAT = 16, 256, 1664, 1024
RING = 96
R, Z = (0, RING), (RING, TOK - RING)
LO, HI, ALL = pl.ds(0, 4), pl.ds(4, 4), pl.ds(0, 8)
CLASSES = (0, 1)
MESSAGES = 106


def whole(part):
    return pl.ds(*part)


def first(part):
    return pl.ds(part[0], part[1] // 2)


def second(part):
    return pl.ds(part[0] + part[1] // 2, part[1] // 2)


def loop(count, step):
    def body(i, carry):
        step(i)
        return carry

    lax.fori_loop(0, count, body, 0)


def by_rows(first, count, step):
    loop(count // ROWS, lambda i: step(pl.ds(pl.multiple_of(first + i * ROWS, ROWS), ROWS)))


def kernel(
    gate_in, up_in, weight_in, grads_in,
    layer_ref, gate_delta, up_delta, down,
    gate, up, weight, hidden, grads, gate_factor, up_factor,
    partial, opposite, direct, crossed, crossed_ring,
    layer, layer_got, layer_sum, layer_opp, layer_dir, layer_crossed, layer_mine,
    send_sem, recv_sem, local_sem,
):
    f, t = lax.axis_index("fsdp"), lax.axis_index("tp")
    zh, y = f // NY, lax.rem(f, NY)
    x, zl, core = t // 4, lax.rem(t // 2, 2), lax.rem(t, 2)

    def group(k, dy):
        return lax.rem(zh + k, 2) * NY + lax.rem(y + dy + NY, NY)

    def share(k, dx):
        return lax.rem(x + dx + NX, NX) * 4 + lax.rem(zl + k, 2) * 2 + core

    y_next, y_prev, z_other = (group(0, 1), t), (group(0, -1), t), (group(1, 0), t)
    x_next, x_prev, z_near = (f, share(0, 1)), (f, share(0, -1)), (f, share(1, 0))
    c_other = (f, t + 1 - 2 * core)

    used = [0]

    def message(src, dst, device):
        i = used[0]
        used[0] += 1
        return pltpu.make_async_remote_copy(
            src, dst, send_sem.at[i], recv_sem.at[i], device_id=device, device_id_type=MESH
        )

    def same(ref, device):
        return message(ref, ref, device)

    h, hz = {}, {}
    for k, part in ((0, Z), (0, R), (1, Z)):
        mine, prev, next_ = group(k, 0), group(k, -1), group(k, 1)
        h[k, part, "p"] = same(hidden.at[mine, whole(part)], y_next)
        h[k, part, "m"] = same(hidden.at[mine, whole(part)], y_prev)
        h[k, part, "pF"] = same(hidden.at[prev, first(part)], y_next)
        h[k, part, "mF"] = same(hidden.at[next_, second(part)], y_prev)
    hz["Z"] = same(hidden.at[f, whole(Z)], z_other)
    for dy in (0, 1, -1, 2):
        hz[dy] = same(hidden.at[group(0, dy), whole(R)], z_other)

    def features(i):
        return pl.ds(pl.multiple_of(i * FEAT, FEAT), FEAT)

    def rows_of(i):
        return pl.ds(pl.multiple_of(i * ROWS, ROWS), ROWS)

    def block(i, groups=ALL):
        return grads.at[groups, rows_of(i)]

    ga = []
    for d in range(1, GROUPS):
        to = lax.rem(f + d, GROUPS)
        ga.append(message(grads_in.at[:, features(to)], grads.at[f, rows_of(t)], (to, t)))
    gz = same(block(t), z_near)
    gx, gc = {}, {}
    for k in (0, 1):
        gx[k, "p"] = same(block(share(k, 0)), x_next)
        gx[k, "m"] = same(block(share(k, 0)), x_prev)
        gx[k, "pF"] = same(block(share(k, -1), LO), x_next)
        gx[k, "mF"] = same(block(share(k, 1), HI), x_prev)
        for dx in (0, -1, 1, 2):
            gc[k, dx] = same(block(share(k, dx)), c_other)

    r = {}
    for n, (k, part) in enumerate(((1, Z), (0, Z), (0, R))):
        far, next_, prev = group(k, 2), group(k, 1), group(k, -1)
        half = pl.ds(0, part[1] // 2)
        r[k, part, "pO"] = message(partial.at[far, first(part)], opposite.at[n, 0, half], y_next)
        r[k, part, "mO"] = message(partial.at[far, second(part)], opposite.at[n, 1, half], y_prev)
        r[k, part, "pI"] = message(partial.at[next_, second(part)], direct.at[k, 0, second(part)], y_next)
        r[k, part, "mI"] = message(partial.at[prev, first(part)], direct.at[k, 1, first(part)], y_prev)
        r[k, part, "pD"] = message(partial.at[next_, first(part)], direct.at[k, 0, first(part)], y_next)
        r[k, part, "mD"] = message(partial.at[prev, second(part)], direct.at[k, 1, second(part)], y_prev)
    rz = [message(partial.at[group(1, 0), rows], crossed.at[rows], z_other) for rows in (first(Z), second(Z))]
    rr = {dy: message(partial.at[group(1, dy), whole(R)], crossed_ring.at[dy % NY], z_other) for dy in (2, 1, -1, 0)}

    core_first = used[0]
    used[0] += GROUPS

    def lc(g):
        return pltpu.make_async_remote_copy(
            layer.at[g, :, :, 1 - core], layer_got.at[g], send_sem.at[core_first + g], recv_sem.at[core_first + g],
            device_id=c_other, device_id_type=MESH,
        )

    def chunk(k, dx, groups=ALL):
        return layer_sum.at[groups, lax.rem(x + dx + NX, NX), lax.rem(zl + k, 2)]

    def of_class(batch, at=0, count=4):
        return pl.ds(lax.rem(zh + batch, 2) * NY + at, count)

    xr, lz = {}, {}
    for b in CLASSES:
        near, far = of_class(b, 0, 2), of_class(b, 2, 2)
        for k in (0, 1):
            xr[b, k, "pO"] = message(chunk(k, 2, near), layer_opp.at[b, k, 0], x_next)
            xr[b, k, "mO"] = message(chunk(k, 2, far), layer_opp.at[b, k, 1], x_prev)
            xr[b, k, "pI"] = message(chunk(k, 1, far), layer_dir.at[k, 0, far], x_next)
            xr[b, k, "mI"] = message(chunk(k, -1, near), layer_dir.at[k, 1, near], x_prev)
            xr[b, k, "pD"] = message(chunk(k, 1, near), layer_dir.at[k, 0, near], x_next)
            xr[b, k, "mD"] = message(chunk(k, -1, far), layer_dir.at[k, 1, far], x_prev)
        lz[b] = message(chunk(1, 0, of_class(b)), layer_crossed.at[of_class(b)], z_near)
    lo = {}
    for d in range(1, GROUPS):
        to = group(d // NY, d % NY)
        lo[d] = message(layer_mine.at[to], layer_ref.at[:, features(f)], (to, t))
    assert used[0] == MESSAGES

    def start(*copies):
        for copy in copies:
            copy.start()

    def got(*copies):
        for copy in copies:
            copy.wait_recv()

    load_gate = pltpu.make_async_copy(gate_in, gate, local_sem.at[0])
    load_up = pltpu.make_async_copy(up_in, up, local_sem.at[1])
    load_weight = pltpu.make_async_copy(weight_in, weight, local_sem.at[2])
    load_grads = pltpu.make_async_copy(grads_in.at[:, features(f)], grads.at[f, rows_of(t)], local_sem.at[3])
    start(load_gate, load_up, load_grads, load_weight)

    barrier = pltpu.get_barrier_semaphore()
    peers = [(lax.rem(f + d, GROUPS), t) for d in range(1, GROUPS)] + [x_next, x_prev, z_near, c_other]
    for peer in peers:
        pl.semaphore_signal(barrier, inc=1, device_id=peer, device_id_type=MESH)
    pl.semaphore_wait(barrier, len(peers))

    start(*ga)

    def activation(rows):
        value = gate[rows].astype(F32)
        hidden[f, rows] = (value * jax.nn.sigmoid(value) * up[rows].astype(F32)).astype(BF16)

    load_gate.wait()
    load_up.wait()
    by_rows(*Z, activation)
    start(hz["Z"], h[0, Z, "p"], h[0, Z, "m"])
    by_rows(*R, activation)
    start(h[0, R, "p"], h[0, R, "m"])

    load_grads.wait()
    got(*ga)
    start(gz, gx[0, "p"], gx[0, "m"], gc[0, 0])

    def factors(rows):
        value = gate[rows].astype(F32)
        sigmoid = jax.nn.sigmoid(value)
        gate_factor[rows] = up[rows].astype(F32) * sigmoid * (1.0 + value * (1.0 - sigmoid))
        up_factor[rows] = value * sigmoid

    def layer_partial(g):
        value = jnp.dot(hidden[g], weight[...], preferred_element_type=F32).astype(BF16)
        layer[g] = value.reshape(4, 2, 2, ROWS, FEAT)
        lc(g).start()

    by_rows(0, TOK, factors)
    load_weight.wait()

    got(gx[0, "p"], gx[0, "m"])
    start(gx[0, "pF"], gx[0, "mF"], gc[0, -1], gc[0, 1])
    got(h[0, Z, "p"], h[0, Z, "m"])
    start(h[0, Z, "pF"], h[0, Z, "mF"])
    got(gz)
    start(gx[1, "p"], gx[1, "m"], gc[1, 0])
    got(hz["Z"])
    start(h[1, Z, "p"], h[1, Z, "m"], hz[0])
    got(gx[0, "pF"], gx[0, "mF"])
    start(gc[0, 2])
    got(h[0, R, "p"], h[0, R, "m"])
    start(h[0, R, "pF"], h[0, R, "mF"], hz[1], hz[-1])

    def layer_early(i):
        layer_partial(lax.rem(zh, 2) * NY + lax.rem(y + jnp.where(i == 0, 0, jnp.where(i == 1, 1, jnp.where(i == 2, 3, 2))), NY))

        @pl.when(i == 2)
        def _():
            got(gx[1, "p"], gx[1, "m"])
            start(gx[1, "pF"], gx[1, "mF"], gc[1, -1], gc[1, 1])
            got(h[0, R, "pF"], h[0, R, "mF"])
            start(hz[2])
            got(h[0, Z, "pF"], h[0, Z, "mF"])

    loop(4, layer_early)
    got(gx[1, "pF"], gx[1, "mF"])
    start(gc[1, 2])
    got(*gc.values())

    def layer_add(b):
        def step(i):
            g = lax.rem(zh + b, 2) * NY + i
            lc(g).wait_recv()
            for at in range(4):
                layer_sum[g, at] = (layer[g, at, :, core].astype(F32) + layer_got[g, at].astype(F32)).astype(BF16)

        loop(4, step)
        start(*[xr[b, k, name] for name in ("pO", "mO", "pI", "mI") for k in (1, 0)])

    def layer_pass_on(b):
        for k in (1, 0):
            for side, dx, at_first, name in ((0, 1, 0, "p"), (1, -1, 2, "m")):
                got(xr[b, k, name + "O"])
                at, z = lax.rem(x + dx + NX, NX), lax.rem(zl + k, 2)
                at_first = lax.rem(zh + b, 2) * NY + at_first

                def step(i, side=side, at_first=at_first, at=at, z=z, k=k):
                    layer_sum[at_first + i, at, z] = (
                        layer_sum[at_first + i, at, z].astype(F32) + layer_opp[b, k, side, i].astype(F32)
                    ).astype(BF16)

                loop(2, step)
                start(xr[b, k, name + "D"])

    def layer_cross(b):
        got(*[xr[b, 1, name] for name in ("pI", "mI", "pD", "mD")])

        def step(i):
            g, z = lax.rem(zh + b, 2) * NY + i, 1 - zl
            layer_sum[g, x, z] = (
                layer_sum[g, x, z].astype(F32) + layer_dir[1, 0, g].astype(F32) + layer_dir[1, 1, g].astype(F32)
            ).astype(BF16)

        loop(4, step)
        start(lz[b])

    def layer_finish(b):
        got(*[xr[b, 0, name] for name in ("pI", "mI", "pD", "mD")], lz[b])

        def step(i):
            g = lax.rem(zh + b, 2) * NY + i
            layer_mine[g] = (
                layer_sum[g, x, zl].astype(F32) + layer_dir[0, 0, g].astype(F32)
                + layer_dir[0, 1, g].astype(F32) + layer_crossed[g].astype(F32)
            ).astype(BF16)

        loop(4, step)
        start(*[lo[d] for d in lo if d // NY == b])

    def hidden_grad(i):
        k, at = 1 - i // 4, lax.rem(i, 4)
        dy = jnp.where(at == 0, 2, jnp.where(at == 1, 1, jnp.where(at == 2, 3, 0)))
        g = lax.rem(zh + k, 2) * NY + lax.rem(y + dy, NY)
        partial[g] = lax.dot_general(
            grads[g], weight[...], (((1,), (1,)), ((), ())), preferred_element_type=F32
        ).astype(BF16)

        @pl.when(i == 0)
        def _():
            start(r[1, Z, "pO"], r[1, Z, "mO"], rr[2])

        @pl.when(i == 1)
        def _():
            start(r[1, Z, "pI"], rr[1])

        @pl.when(i == 2)
        def _():
            start(r[1, Z, "mI"], rr[-1])

        @pl.when(i == 3)
        def _():
            start(rr[0])

        @pl.when(i == 4)
        def _():
            layer_add(0)

    loop(8, hidden_grad)
    got(h[1, Z, "p"], h[1, Z, "m"])
    start(h[1, Z, "pF"], h[1, Z, "mF"])

    def add_into(target, source, at, count):
        def step(i):
            rows = pl.ds(pl.multiple_of(at + i * ROWS, ROWS), ROWS)
            other = pl.ds(pl.multiple_of(i * ROWS, ROWS), ROWS)
            partial[target, rows] = (partial[target, rows].astype(F32) + source[other].astype(F32)).astype(BF16)

        loop(count // ROWS, step)

    def pass_on(n, k, part):
        half = part[1] // 2
        got(r[k, part, "pO"])
        add_into(group(k, 1), opposite.at[n, 0], part[0], half)
        start(r[k, part, "pD"])
        got(r[k, part, "mO"])
        add_into(group(k, -1), opposite.at[n, 1], part[0] + half, half)
        start(r[k, part, "mD"])

    start(r[0, Z, "pO"], r[0, Z, "mO"])
    layer_pass_on(0)
    pass_on(0, 1, Z)
    start(r[0, Z, "pI"], r[0, Z, "mI"])

    got(h[1, Z, "pF"], h[1, Z, "mF"], *[hz[dy] for dy in (0, 1, -1, 2)])
    loop(4, lambda i: layer_partial(lax.rem(zh + 1, 2) * NY + i))
    layer_cross(0)
    pass_on(1, 0, Z)
    layer_add(1)

    def ring_add(dy):
        got(rr[dy])
        add_into(group(0, dy), crossed_ring.at[dy % NY], R[0], R[1])

    def cross():
        mine = group(1, 0)
        for copy, rows, names in ((rz[0], first(Z), ("pD", "mI")), (rz[1], second(Z), ("pI", "mD"))):
            got(*[r[1, Z, name] for name in names])

            def step(at):
                partial[mine, at] = (
                    partial[mine, at].astype(F32) + direct[1, 0, at].astype(F32) + direct[1, 1, at].astype(F32)
                ).astype(BF16)

            by_rows(rows.start, rows.size, step)
            start(copy)

    def down_strip(i):
        units = pl.ds(pl.multiple_of(i * 128, 128), 128)
        total = jnp.zeros((128, FEAT), F32)
        for g in range(GROUPS):
            total += lax.dot_general(
                hidden[g, :, units], grads[g], (((0,), (0,)), ((), ())), preferred_element_type=F32
            )
        down[units] = total.astype(BF16)

        @pl.when(i == 1)
        def _():
            ring_add(2)
            start(r[0, R, "pO"], r[0, R, "mO"])

        @pl.when(i == 3)
        def _():
            layer_pass_on(1)

        @pl.when(i == 5)
        def _():
            cross()
            ring_add(1)
            start(r[0, R, "pI"])
            ring_add(-1)
            start(r[0, R, "mI"])

        @pl.when(i == 7)
        def _():
            layer_finish(0)

        @pl.when(i == 9)
        def _():
            layer_cross(1)

        @pl.when(i == 11)
        def _():
            pass_on(2, 0, R)

    loop(13, down_strip)
    layer_finish(1)
    store_layer = pltpu.make_async_copy(layer_mine.at[f], layer_ref.at[:, features(f)], local_sem.at[4])
    store_layer.start()

    got(rr[0])

    def finish(part, rows):
        def step(i):
            at = pl.ds(pl.multiple_of(rows.start + i * ROWS, ROWS), ROWS)
            total = partial[f, at].astype(F32) + direct[0, 0, at].astype(F32) + direct[0, 1, at].astype(F32)
            if part is R:
                total += crossed_ring[0, at].astype(F32)
            else:
                total += crossed[at].astype(F32)
            gate_delta[at] = (total * gate_factor[at]).astype(BF16)
            up_delta[at] = (total * up_factor[at]).astype(BF16)

        loop(rows.size // ROWS, step)

    got(*[r[0, Z, name] for name in ("pI", "mI", "pD", "mD")], *rz)
    finish(Z, whole(Z))
    got(*[r[0, R, name] for name in ("pI", "mI", "pD", "mD")])
    finish(R, whole(R))

    got(*lo.values())
    for copy in [*h.values(), *hz.values(), *ga, gz, *gx.values(), *gc.values(), *r.values(), *rz, *rr.values(), *xr.values(), *lz.values(), *lo.values()]:
        copy.wait_send()
    loop(GROUPS, lambda g: lc(g).wait_send())
    store_layer.wait()


def hand_over(*refs):
    sources, targets, sem = refs[:4], refs[4:8], refs[8]
    copies = [pltpu.make_async_copy(a, b, sem.at[i]) for i, (a, b) in enumerate(zip(sources, targets))]
    for copy in copies:
        copy.start()
    for copy in copies:
        copy.wait()


def body(gate_pre, up_pre, down_weight, out_grad):
    anywhere = pl.BlockSpec(memory_space=pl.ANY)
    v = pltpu.VMEM
    outs = pl.pallas_call(
        kernel,
        name="feed_forward",
        out_shape=(
            v(out_grad.shape, BF16),
            v(gate_pre.shape, BF16),
            v(up_pre.shape, BF16),
            v(down_weight.shape, BF16),
        ),
        in_specs=[anywhere] * 4,
        out_specs=[pl.BlockSpec(memory_space=v)] * 4,
        scratch_shapes=[
            v((TOK, UNITS), BF16),
            v((TOK, UNITS), BF16),
            v((UNITS, FEAT), BF16),
            v((GROUPS, TOK, UNITS), BF16),
            v((GROUPS, TOK, FEAT), BF16),
            v((TOK, UNITS), F32),
            v((TOK, UNITS), F32),
            v((GROUPS, TOK, UNITS), BF16),
            v((3, 2, Z[1] // 2, UNITS), BF16),
            v((2, 2, TOK, UNITS), BF16),
            v((TOK, UNITS), BF16),
            v((NY, RING, UNITS), BF16),
            v((GROUPS, 4, 2, 2, ROWS, FEAT), BF16),
            v((GROUPS, 4, 2, ROWS, FEAT), BF16),
            v((GROUPS, 4, 2, ROWS, FEAT), BF16),
            v((2, 2, 2, 2, ROWS, FEAT), BF16),
            v((2, 2, GROUPS, ROWS, FEAT), BF16),
            v((GROUPS, ROWS, FEAT), BF16),
            v((GROUPS, ROWS, FEAT), BF16),
            pltpu.SemaphoreType.DMA((MESSAGES,)),
            pltpu.SemaphoreType.DMA((MESSAGES,)),
            pltpu.SemaphoreType.DMA((5,)),
        ],
        compiler_params=pltpu.CompilerParams(
            collective_id=0, has_side_effects=True, vmem_limit_bytes=54 << 20
        ),
        cost_estimate=pl.CostEstimate(flops=21_000_000_000, bytes_accessed=12_000_000, transcendentals=400_000),
    )(gate_pre, up_pre, down_weight, out_grad)
    return pl.pallas_call(
        hand_over,
        name="hand_over",
        out_shape=tuple(jax.ShapeDtypeStruct(out.shape, BF16) for out in outs),
        in_specs=[anywhere] * 4,
        out_specs=[anywhere] * 4,
        scratch_shapes=[pltpu.SemaphoreType.DMA((4,))],
        compiler_params=pltpu.CompilerParams(vmem_limit_bytes=1 << 20),
        cost_estimate=pl.CostEstimate(flops=0, bytes_accessed=12_000_000, transcendentals=0),
    )(*outs)


def solution(mesh):
    return jax.shard_map(
        body,
        mesh=mesh,
        in_specs=(P("fsdp", "tp"), P("fsdp", "tp"), P("tp", "fsdp"), P(("fsdp", "tp"), None)),
        out_specs=(P(("fsdp", "tp"), None), P("fsdp", "tp"), P("fsdp", "tp"), P("tp", "fsdp")),
        check_vma=False,
    )
```

```python
import jax
import jax.numpy as jnp
from jax import lax
from jax.experimental import pallas as pl
from jax.experimental.pallas import tpu as pltpu
from jax.sharding import PartitionSpec as P

MESH = pl.DeviceIdType.MESH
BF16, F32 = jnp.bfloat16, jnp.float32
NY, NX = 4, 4
GROUPS, SHARES = 8, 16
ROWS, TOK, UNITS, FEAT = 16, 256, 1664, 1024
RING = 96
R, Z = (0, RING), (RING, TOK - RING)
LO, HI, ALL = pl.ds(0, 4), pl.ds(4, 4), pl.ds(0, 8)
CLASSES = (0, 1)
MESSAGES = 106


def whole(part):
    return pl.ds(*part)


def first(part):
    return pl.ds(part[0], part[1] // 2)


def second(part):
    return pl.ds(part[0] + part[1] // 2, part[1] // 2)


def loop(count, step):
    def body(i, carry):
        step(i)
        return carry

    lax.fori_loop(0, count, body, 0)


def by_rows(first, count, step):
    loop(count // ROWS, lambda i: step(pl.ds(pl.multiple_of(first + i * ROWS, ROWS), ROWS)))


def kernel(
    gate_in, up_in, weight_in, grads_in,
    layer_ref, gate_delta, up_delta, down,
    gate, up, weight, hidden, grads, gate_factor, up_factor,
    partial, opposite, direct, crossed, crossed_ring,
    layer, layer_got, layer_sum, layer_opp, layer_dir, layer_crossed, layer_mine,
    send_sem, recv_sem, local_sem,
):
    f, t = lax.axis_index("fsdp"), lax.axis_index("tp")
    zh, y = f // NY, lax.rem(f, NY)
    x, zl, core = t // 4, lax.rem(t // 2, 2), lax.rem(t, 2)

    def group(k, dy):
        return lax.rem(zh + k, 2) * NY + lax.rem(y + dy + NY, NY)

    def share(k, dx):
        return lax.rem(x + dx + NX, NX) * 4 + lax.rem(zl + k, 2) * 2 + core

    y_next, y_prev, z_other = (group(0, 1), t), (group(0, -1), t), (group(1, 0), t)
    x_next, x_prev, z_near = (f, share(0, 1)), (f, share(0, -1)), (f, share(1, 0))
    c_other = (f, t + 1 - 2 * core)

    used = [0]

    def message(src, dst, device):
        i = used[0]
        used[0] += 1
        return pltpu.make_async_remote_copy(
            src, dst, send_sem.at[i], recv_sem.at[i], device_id=device, device_id_type=MESH
        )

    def same(ref, device):
        return message(ref, ref, device)

    h, hz = {}, {}
    for k, part in ((0, Z), (0, R), (1, Z)):
        mine, prev, next_ = group(k, 0), group(k, -1), group(k, 1)
        h[k, part, "p"] = same(hidden.at[mine, whole(part)], y_next)
        h[k, part, "m"] = same(hidden.at[mine, whole(part)], y_prev)
        h[k, part, "pF"] = same(hidden.at[prev, first(part)], y_next)
        h[k, part, "mF"] = same(hidden.at[next_, second(part)], y_prev)
    hz["Z"] = same(hidden.at[f, whole(Z)], z_other)
    for dy in (0, 1, -1, 2):
        hz[dy] = same(hidden.at[group(0, dy), whole(R)], z_other)

    def features(i):
        return pl.ds(pl.multiple_of(i * FEAT, FEAT), FEAT)

    def rows_of(i):
        return pl.ds(pl.multiple_of(i * ROWS, ROWS), ROWS)

    def block(i, groups=ALL):
        return grads.at[groups, rows_of(i)]

    ga = []
    for d in range(1, GROUPS):
        to = lax.rem(f + d, GROUPS)
        ga.append(message(grads_in.at[:, features(to)], grads.at[f, rows_of(t)], (to, t)))
    gz = same(block(t), z_near)
    gx, gc = {}, {}
    for k in (0, 1):
        gx[k, "p"] = same(block(share(k, 0)), x_next)
        gx[k, "m"] = same(block(share(k, 0)), x_prev)
        gx[k, "pF"] = same(block(share(k, -1), LO), x_next)
        gx[k, "mF"] = same(block(share(k, 1), HI), x_prev)
        for dx in (0, -1, 1, 2):
            gc[k, dx] = same(block(share(k, dx)), c_other)

    r = {}
    for n, (k, part) in enumerate(((1, Z), (0, Z), (0, R))):
        far, next_, prev = group(k, 2), group(k, 1), group(k, -1)
        half = pl.ds(0, part[1] // 2)
        r[k, part, "pO"] = message(partial.at[far, first(part)], opposite.at[n, 0, half], y_next)
        r[k, part, "mO"] = message(partial.at[far, second(part)], opposite.at[n, 1, half], y_prev)
        r[k, part, "pI"] = message(partial.at[next_, second(part)], direct.at[k, 0, second(part)], y_next)
        r[k, part, "mI"] = message(partial.at[prev, first(part)], direct.at[k, 1, first(part)], y_prev)
        r[k, part, "pD"] = message(partial.at[next_, first(part)], direct.at[k, 0, first(part)], y_next)
        r[k, part, "mD"] = message(partial.at[prev, second(part)], direct.at[k, 1, second(part)], y_prev)
    rz = [message(partial.at[group(1, 0), rows], crossed.at[rows], z_other) for rows in (first(Z), second(Z))]
    rr = {dy: message(partial.at[group(1, dy), whole(R)], crossed_ring.at[dy % NY], z_other) for dy in (2, 1, -1, 0)}

    core_first = used[0]
    used[0] += GROUPS

    def lc(g):
        return pltpu.make_async_remote_copy(
            layer.at[g, :, :, 1 - core], layer_got.at[g], send_sem.at[core_first + g], recv_sem.at[core_first + g],
            device_id=c_other, device_id_type=MESH,
        )

    def chunk(k, dx, groups=ALL):
        return layer_sum.at[groups, lax.rem(x + dx + NX, NX), lax.rem(zl + k, 2)]

    def of_class(batch, at=0, count=4):
        return pl.ds(lax.rem(zh + batch, 2) * NY + at, count)

    xr, lz = {}, {}
    for b in CLASSES:
        near, far = of_class(b, 0, 2), of_class(b, 2, 2)
        for k in (0, 1):
            xr[b, k, "pO"] = message(chunk(k, 2, near), layer_opp.at[b, k, 0], x_next)
            xr[b, k, "mO"] = message(chunk(k, 2, far), layer_opp.at[b, k, 1], x_prev)
            xr[b, k, "pI"] = message(chunk(k, 1, far), layer_dir.at[k, 0, far], x_next)
            xr[b, k, "mI"] = message(chunk(k, -1, near), layer_dir.at[k, 1, near], x_prev)
            xr[b, k, "pD"] = message(chunk(k, 1, near), layer_dir.at[k, 0, near], x_next)
            xr[b, k, "mD"] = message(chunk(k, -1, far), layer_dir.at[k, 1, far], x_prev)
        lz[b] = message(chunk(1, 0, of_class(b)), layer_crossed.at[of_class(b)], z_near)
    lo = {}
    for d in range(1, GROUPS):
        to = group(d // NY, d % NY)
        lo[d] = message(layer_mine.at[to], layer_ref.at[:, features(f)], (to, t))
    assert used[0] == MESSAGES

    def start(*copies):
        for copy in copies:
            copy.start()

    def got(*copies):
        for copy in copies:
            copy.wait_recv()

    load_gate = pltpu.make_async_copy(gate_in, gate, local_sem.at[0])
    load_up = pltpu.make_async_copy(up_in, up, local_sem.at[1])
    load_weight = pltpu.make_async_copy(weight_in, weight, local_sem.at[2])
    load_grads = pltpu.make_async_copy(grads_in.at[:, features(f)], grads.at[f, rows_of(t)], local_sem.at[3])
    start(load_gate, load_up, load_grads, load_weight)

    barrier = pltpu.get_barrier_semaphore()
    peers = [(lax.rem(f + d, GROUPS), t) for d in range(1, GROUPS)] + [x_next, x_prev, z_near, c_other]
    for peer in peers:
        pl.semaphore_signal(barrier, inc=1, device_id=peer, device_id_type=MESH)
    pl.semaphore_wait(barrier, len(peers))

    start(*ga)

    def activation(rows):
        value = gate[rows].astype(F32)
        hidden[f, rows] = (value * jax.nn.sigmoid(value) * up[rows].astype(F32)).astype(BF16)

    load_gate.wait()
    load_up.wait()
    by_rows(*Z, activation)
    start(hz["Z"], h[0, Z, "p"], h[0, Z, "m"])
    by_rows(*R, activation)
    start(h[0, R, "p"], h[0, R, "m"])

    load_grads.wait()
    got(*ga)
    start(gz, gx[0, "p"], gx[0, "m"], gc[0, 0])

    def factors(rows):
        value = gate[rows].astype(F32)
        sigmoid = jax.nn.sigmoid(value)
        gate_factor[rows] = up[rows].astype(F32) * sigmoid * (1.0 + value * (1.0 - sigmoid))
        up_factor[rows] = value * sigmoid

    def layer_partial(g):
        value = jnp.dot(hidden[g], weight[...], preferred_element_type=F32).astype(BF16)
        layer[g] = value.reshape(4, 2, 2, ROWS, FEAT)
        lc(g).start()

    by_rows(0, TOK, factors)
    load_weight.wait()

    got(gx[0, "p"], gx[0, "m"])
    start(gx[0, "pF"], gx[0, "mF"], gc[0, -1], gc[0, 1])
    got(gz)
    start(gx[1, "p"], gx[1, "m"], gc[1, 0])
    got(hz["Z"])
    start(h[1, Z, "p"], h[1, Z, "m"], hz[0])
    got(h[0, Z, "p"], h[0, Z, "m"])
    start(h[0, Z, "pF"], h[0, Z, "mF"])
    got(gx[0, "pF"], gx[0, "mF"])
    start(gc[0, 2])
    got(h[0, R, "p"], h[0, R, "m"])
    start(h[0, R, "pF"], h[0, R, "mF"], hz[1], hz[-1])

    def layer_early(i):
        layer_partial(lax.rem(zh, 2) * NY + lax.rem(y + jnp.where(i == 0, 0, jnp.where(i == 1, 1, jnp.where(i == 2, 3, 2))), NY))

        @pl.when(i == 2)
        def _():
            got(gx[1, "p"], gx[1, "m"])
            start(gx[1, "pF"], gx[1, "mF"], gc[1, -1], gc[1, 1])
            got(h[0, R, "pF"], h[0, R, "mF"])
            start(hz[2])
            got(h[0, Z, "pF"], h[0, Z, "mF"])

    loop(4, layer_early)
    got(gx[1, "pF"], gx[1, "mF"])
    start(gc[1, 2])
    got(*gc.values())

    def layer_add(b):
        def step(i):
            g = lax.rem(zh + b, 2) * NY + i
            lc(g).wait_recv()
            for at in range(4):
                layer_sum[g, at] = (layer[g, at, :, core].astype(F32) + layer_got[g, at].astype(F32)).astype(BF16)

        loop(4, step)
        start(*[xr[b, k, name] for name in ("pO", "mO", "pI", "mI") for k in (1, 0)])

    def layer_pass_on(b):
        for k in (1, 0):
            for side, dx, at_first, name in ((0, 1, 0, "p"), (1, -1, 2, "m")):
                got(xr[b, k, name + "O"])
                at, z = lax.rem(x + dx + NX, NX), lax.rem(zl + k, 2)
                at_first = lax.rem(zh + b, 2) * NY + at_first

                def step(i, side=side, at_first=at_first, at=at, z=z, k=k):
                    layer_sum[at_first + i, at, z] = (
                        layer_sum[at_first + i, at, z].astype(F32) + layer_opp[b, k, side, i].astype(F32)
                    ).astype(BF16)

                loop(2, step)
                start(xr[b, k, name + "D"])

    def layer_cross(b):
        got(*[xr[b, 1, name] for name in ("pI", "mI", "pD", "mD")])

        def step(i):
            g, z = lax.rem(zh + b, 2) * NY + i, 1 - zl
            layer_sum[g, x, z] = (
                layer_sum[g, x, z].astype(F32) + layer_dir[1, 0, g].astype(F32) + layer_dir[1, 1, g].astype(F32)
            ).astype(BF16)

        loop(4, step)
        start(lz[b])

    def layer_finish(b):
        got(*[xr[b, 0, name] for name in ("pI", "mI", "pD", "mD")], lz[b])

        def step(i):
            g = lax.rem(zh + b, 2) * NY + i
            layer_mine[g] = (
                layer_sum[g, x, zl].astype(F32) + layer_dir[0, 0, g].astype(F32)
                + layer_dir[0, 1, g].astype(F32) + layer_crossed[g].astype(F32)
            ).astype(BF16)

        loop(4, step)
        start(*[lo[d] for d in lo if d // NY == b])

    def hidden_grad(i):
        k, at = 1 - i // 4, lax.rem(i, 4)
        dy = jnp.where(at == 0, 2, jnp.where(at == 1, 1, jnp.where(at == 2, 3, 0)))
        g = lax.rem(zh + k, 2) * NY + lax.rem(y + dy, NY)
        partial[g] = lax.dot_general(
            grads[g], weight[...], (((1,), (1,)), ((), ())), preferred_element_type=F32
        ).astype(BF16)

        @pl.when(i == 0)
        def _():
            start(r[1, Z, "pO"], r[1, Z, "mO"], rr[2])

        @pl.when(i == 1)
        def _():
            start(r[1, Z, "pI"], rr[1])

        @pl.when(i == 2)
        def _():
            start(r[1, Z, "mI"], rr[-1])

        @pl.when(i == 3)
        def _():
            start(rr[0])

        @pl.when(i == 4)
        def _():
            layer_add(0)

    loop(8, hidden_grad)
    got(h[1, Z, "p"], h[1, Z, "m"])
    start(h[1, Z, "pF"], h[1, Z, "mF"])

    def add_into(target, source, at, count):
        def step(i):
            rows = pl.ds(pl.multiple_of(at + i * ROWS, ROWS), ROWS)
            other = pl.ds(pl.multiple_of(i * ROWS, ROWS), ROWS)
            partial[target, rows] = (partial[target, rows].astype(F32) + source[other].astype(F32)).astype(BF16)

        loop(count // ROWS, step)

    def pass_on(n, k, part):
        half = part[1] // 2
        got(r[k, part, "pO"])
        add_into(group(k, 1), opposite.at[n, 0], part[0], half)
        start(r[k, part, "pD"])
        got(r[k, part, "mO"])
        add_into(group(k, -1), opposite.at[n, 1], part[0] + half, half)
        start(r[k, part, "mD"])

    start(r[0, Z, "pO"], r[0, Z, "mO"])
    layer_pass_on(0)
    pass_on(0, 1, Z)
    start(r[0, Z, "pI"], r[0, Z, "mI"])

    got(h[1, Z, "pF"], h[1, Z, "mF"], *[hz[dy] for dy in (0, 1, -1, 2)])
    loop(4, lambda i: layer_partial(lax.rem(zh + 1, 2) * NY + i))
    layer_cross(0)
    pass_on(1, 0, Z)
    layer_add(1)

    def ring_add(dy):
        got(rr[dy])
        add_into(group(0, dy), crossed_ring.at[dy % NY], R[0], R[1])

    def cross():
        mine = group(1, 0)
        for copy, rows, names in ((rz[0], first(Z), ("pD", "mI")), (rz[1], second(Z), ("pI", "mD"))):
            got(*[r[1, Z, name] for name in names])

            def step(at):
                partial[mine, at] = (
                    partial[mine, at].astype(F32) + direct[1, 0, at].astype(F32) + direct[1, 1, at].astype(F32)
                ).astype(BF16)

            by_rows(rows.start, rows.size, step)
            start(copy)

    def down_strip(i):
        units = pl.ds(pl.multiple_of(i * 128, 128), 128)
        total = jnp.zeros((128, FEAT), F32)
        for g in range(GROUPS):
            total += lax.dot_general(
                hidden[g, :, units], grads[g], (((0,), (0,)), ((), ())), preferred_element_type=F32
            )
        down[units] = total.astype(BF16)

        @pl.when(i == 1)
        def _():
            ring_add(2)
            start(r[0, R, "pO"], r[0, R, "mO"])

        @pl.when(i == 3)
        def _():
            layer_pass_on(1)

        @pl.when(i == 5)
        def _():
            cross()
            ring_add(1)
            start(r[0, R, "pI"])
            ring_add(-1)
            start(r[0, R, "mI"])

        @pl.when(i == 7)
        def _():
            layer_finish(0)

        @pl.when(i == 9)
        def _():
            layer_cross(1)

        @pl.when(i == 11)
        def _():
            pass_on(2, 0, R)

    loop(13, down_strip)
    layer_finish(1)
    store_layer = pltpu.make_async_copy(layer_mine.at[f], layer_ref.at[:, features(f)], local_sem.at[4])
    store_layer.start()

    got(rr[0])

    def finish(part, rows):
        def step(i):
            at = pl.ds(pl.multiple_of(rows.start + i * ROWS, ROWS), ROWS)
            total = partial[f, at].astype(F32) + direct[0, 0, at].astype(F32) + direct[0, 1, at].astype(F32)
            if part is R:
                total += crossed_ring[0, at].astype(F32)
            else:
                total += crossed[at].astype(F32)
            gate_delta[at] = (total * gate_factor[at]).astype(BF16)
            up_delta[at] = (total * up_factor[at]).astype(BF16)

        loop(rows.size // ROWS, step)

    got(*[r[0, Z, name] for name in ("pI", "mI", "pD", "mD")], *rz)
    finish(Z, whole(Z))
    got(*[r[0, R, name] for name in ("pI", "mI", "pD", "mD")])
    finish(R, whole(R))

    got(*lo.values())
    for copy in [*h.values(), *hz.values(), *ga, gz, *gx.values(), *gc.values(), *r.values(), *rz, *rr.values(), *xr.values(), *lz.values(), *lo.values()]:
        copy.wait_send()
    loop(GROUPS, lambda g: lc(g).wait_send())
    store_layer.wait()


def hand_over(*refs):
    sources, targets, sem = refs[:4], refs[4:8], refs[8]
    copies = [pltpu.make_async_copy(a, b, sem.at[i]) for i, (a, b) in enumerate(zip(sources, targets))]
    for copy in copies:
        copy.start()
    for copy in copies:
        copy.wait()


def body(gate_pre, up_pre, down_weight, out_grad):
    anywhere = pl.BlockSpec(memory_space=pl.ANY)
    v = pltpu.VMEM
    outs = pl.pallas_call(
        kernel,
        name="feed_forward",
        out_shape=(
            v(out_grad.shape, BF16),
            v(gate_pre.shape, BF16),
            v(up_pre.shape, BF16),
            v(down_weight.shape, BF16),
        ),
        in_specs=[anywhere] * 4,
        out_specs=[pl.BlockSpec(memory_space=v)] * 4,
        scratch_shapes=[
            v((TOK, UNITS), BF16),
            v((TOK, UNITS), BF16),
            v((UNITS, FEAT), BF16),
            v((GROUPS, TOK, UNITS), BF16),
            v((GROUPS, TOK, FEAT), BF16),
            v((TOK, UNITS), F32),
            v((TOK, UNITS), F32),
            v((GROUPS, TOK, UNITS), BF16),
            v((3, 2, Z[1] // 2, UNITS), BF16),
            v((2, 2, TOK, UNITS), BF16),
            v((TOK, UNITS), BF16),
            v((NY, RING, UNITS), BF16),
            v((GROUPS, 4, 2, 2, ROWS, FEAT), BF16),
            v((GROUPS, 4, 2, ROWS, FEAT), BF16),
            v((GROUPS, 4, 2, ROWS, FEAT), BF16),
            v((2, 2, 2, 2, ROWS, FEAT), BF16),
            v((2, 2, GROUPS, ROWS, FEAT), BF16),
            v((GROUPS, ROWS, FEAT), BF16),
            v((GROUPS, ROWS, FEAT), BF16),
            pltpu.SemaphoreType.DMA((MESSAGES,)),
            pltpu.SemaphoreType.DMA((MESSAGES,)),
            pltpu.SemaphoreType.DMA((5,)),
        ],
        compiler_params=pltpu.CompilerParams(
            collective_id=0, has_side_effects=True, vmem_limit_bytes=54 << 20
        ),
        cost_estimate=pl.CostEstimate(flops=21_000_000_000, bytes_accessed=12_000_000, transcendentals=400_000),
    )(gate_pre, up_pre, down_weight, out_grad)
    return pl.pallas_call(
        hand_over,
        name="hand_over",
        out_shape=tuple(jax.ShapeDtypeStruct(out.shape, BF16) for out in outs),
        in_specs=[anywhere] * 4,
        out_specs=[anywhere] * 4,
        scratch_shapes=[pltpu.SemaphoreType.DMA((4,))],
        compiler_params=pltpu.CompilerParams(vmem_limit_bytes=1 << 20),
        cost_estimate=pl.CostEstimate(flops=0, bytes_accessed=12_000_000, transcendentals=0),
    )(*outs)


def solution(mesh):
    return jax.shard_map(
        body,
        mesh=mesh,
        in_specs=(P("fsdp", "tp"), P("fsdp", "tp"), P("tp", "fsdp"), P(("fsdp", "tp"), None)),
        out_specs=(P(("fsdp", "tp"), None), P("fsdp", "tp"), P("fsdp", "tp"), P("tp", "fsdp")),
        check_vma=False,
    )
```
